256 devices in a mesh: blk: 32 (over z, y_hi, core), group: 8 (over y_lo, x).
Axes of the slice: x: 4, y: 4 (y_hi: 2, y_lo: 2; y = y_hi * 2 + y_lo), z: 8, core: 2. Of those that a mesh axis runs over, the one named last changes fastest.
Arguments:
- images: bfloat16 [32768, 1152], P(('blk', 'group')), may hold values from -6 to 6
- texts: bfloat16 [32768, 1152], P(('blk', 'group')), may hold values from -6 to 6
- logit_scale: float32 [1], replicated, may hold values from 1 to 4
- logit_bias: float32 [1], replicated, may hold values from -4 to -1
Outputs:
- grad_images: float32 [32768, 1152], P(('blk', 'group'))
- grad_texts: float32 [32768, 1152], P(('blk', 'group'))
- loss: float32 [1], replicated
The draws below stay inside these ranges and needn't reach their ends.
All inputs are finite; a program needn't handle non-finite values.
Results may differ from the reference program's by a relative error of at most 0.0015.
Values may be sent and summed in bfloat16 or wider, within the bound.
No kernel may reach another device: no remote copies, remote signals or barrier semaphores. Data moves between devices by JAX's collectives and lax.ppermute only.
A program may use at most 64 MiB of HBM per device.

```python
import math
import jax
import jax.numpy as jnp
from jax import lax

D = 1152
STEPS = 8
GROUP_ROWS = 1024
PAIRS = 32768


def levels(own_key, shape, cuts, low, top_value):
    gain = 1.0
    for position, blocks in cuts:
        draws = jax.random.uniform(jax.random.fold_in(jax.random.fold_in(own_key, 6), position), (blocks,), jnp.float32, low / len(cuts), top_value / len(cuts))
        gain = gain * jnp.repeat(jnp.exp(draws), shape[position] // blocks).reshape((-1,) + (1,) * (len(shape) - 1 - position))
    return gain


def bell_draw(stream_key, extent, spread, most, pieces=(), held_as=jnp.bfloat16):
    drawn = spread * jax.random.normal(stream_key, extent, jnp.float32)
    if pieces:
        drawn = drawn * levels(stream_key, extent, pieces, -0.22, 0.18)
    return jnp.clip(drawn, -most, most).astype(held_as)


def setup_inputs(seed: int = 0) -> dict:
    arg_keys = jax.random.split(jax.random.key(seed), 5)
    return {
        "images": bell_draw(arg_keys[0], (PAIRS, D), 1.0, 6.0, ((0, 256),)),
        "texts": bell_draw(arg_keys[1], (PAIRS, D), 1.0, 6.0, ((0, 256),)),
        "logit_scale": jnp.clip(jnp.exp(jax.random.uniform(arg_keys[2], (1,), jnp.float32, math.log(1.0), math.log(4.0))), 1.0, 4.0),
        "logit_bias": jnp.clip(jax.random.uniform(arg_keys[3], (1,), jnp.float32, -4.0, -1.0), -4.0, -1.0),
    }


def reference(images, texts, logit_scale, logit_bias):
    blocks = PAIRS // GROUP_ROWS
    left = images.astype(jnp.float32).reshape(blocks, GROUP_ROWS, D)
    right = texts.astype(jnp.float32).reshape(blocks, GROUP_ROWS, D)
    factor = logit_scale[0] / math.sqrt(D)
    weight = factor / math.sqrt(STEPS * GROUP_ROWS)
    diagonal = jnp.eye(GROUP_ROWS, dtype=jnp.float32)
    grad_left = jnp.zeros((blocks, GROUP_ROWS, D), jnp.float32)
    grad_right = jnp.zeros((blocks, GROUP_ROWS, D), jnp.float32)
    total = jnp.float32(0.0)
    for offset in range(STEPS):
        moved = jnp.roll(right, offset, axis=0)
        logits = jnp.einsum('bid,bjd->bij', left, moved) * factor + logit_bias[0]
        if offset == 0:
            signs = 2.0 * diagonal - 1.0
        else:
            signs = -jnp.ones_like(diagonal)
        total = total + jnp.sum(jax.nn.softplus(-signs * logits))
        coef = (-signs * jax.nn.sigmoid(-signs * logits) * weight).astype(jnp.bfloat16)
        coef = lax.optimization_barrier(coef).astype(jnp.float32)
        grad_left = grad_left + jnp.einsum('bij,bjd->bid', coef, moved)
        grad_right = grad_right + jnp.roll(jnp.einsum('bij,bid->bjd', coef, left), -offset, axis=0)
    loss = (total / PAIRS).reshape(1)
    return (grad_left.reshape(PAIRS, D), grad_right.reshape(PAIRS, D), loss)
```

```python
import math

import jax
import jax.numpy as jnp
from jax import lax
from jax.experimental import pallas as pl
from jax.experimental.pallas import tpu as pltpu
from jax.sharding import PartitionSpec as P

STEPS = 8
TILE = 256
CODE_SCALE = 2.0**36
CODE_FLOOR = 2.0**-126


def encode(value):
    scaled = value * CODE_SCALE
    return (scaled * scaled * scaled).astype(jnp.bfloat16)


def decode(code):
    wide = code.astype(jnp.float32)
    size = jnp.abs(wide)
    root = jnp.exp2(jnp.log2(jnp.maximum(size, CODE_FLOOR)) * (1.0 / 3.0)) * (1.0 / CODE_SCALE)
    root = jnp.where(size < CODE_FLOOR, 0.0, root)
    return jnp.where(wide < 0, -root, root)


def shift_blk(value, even, odd):
    count = lax.axis_size("blk")
    pairs = [(s, (s + (odd if s % 2 else even)) % count) for s in range(count)]
    return lax.ppermute(value, "blk", pairs)


def swap_core(value):
    return shift_blk(value, 1, -1)


def shift_group(value, over_y, over_x):
    pairs = [(s, ((s // 4 + over_y) % 2) * 4 + (s + over_x) % 4) for s in range(8)]
    return lax.ppermute(value, "group", pairs)


def sum_over(value, axis, first, count):
    size = lax.axis_size(axis)
    terms = [value] + [
        lax.ppermute(value, axis, [(s, s ^ (first * j)) for s in range(size)]) for j in range(1, count)
    ]
    while len(terms) > 1:
        terms = [a + b for a, b in zip(terms[::2], terms[1::2])]
    return terms[0]


def kernel(scalars, *refs):
    image_refs, text_refs = refs[:8], refs[8:16]
    gi_own, gi_codes = refs[16], refs[17:24]
    gt_wide, gt_codes = refs[24:28], refs[28:32]
    loss_ref = refs[32]
    images, texts, text_acc, coef, gi_wide, gi_stage, gt_stage, loss_acc, in_sems, out_sems = refs[33:]
    rows = image_refs[0].shape[0]
    total = 8 * rows
    width = images.shape[1]

    def fetch(i):
        source, place = (image_refs[i], images) if i < 8 else (text_refs[i - 8], texts)
        return pltpu.make_async_copy(source, place.at[pl.ds((i % 8) * rows, rows), :], in_sems.at[i])

    for i in range(8):
        fetch(8 + i).start()
    for i in range(8):
        fetch(i).start()
    for i in range(16):
        fetch(i).wait()
    factor, bias, weight = scalars[0], scalars[1], scalars[2]
    loss_acc[...] = jnp.zeros_like(loss_acc)
    text_acc[...] = jnp.zeros_like(text_acc)

    def step(ic, _):
        at = pl.ds(pl.multiple_of(ic * TILE, TILE), TILE)
        left = images[at, :]
        for tc in range(total // TILE):
            right = texts[tc * TILE : (tc + 1) * TILE, :]
            logits = lax.dot_general(left, right, (((1,), (1,)), ((), ())), preferred_element_type=jnp.float32)
            logits = logits * factor + bias
            if tc == 0:
                row = lax.broadcasted_iota(jnp.int32, (TILE, TILE), 0) + ic * TILE
                col = lax.broadcasted_iota(jnp.int32, (TILE, TILE), 1)
                positive = jnp.logical_and(row == col, col < rows)
                logits = jnp.where(positive, -logits, logits)
            small = jnp.exp(-jnp.abs(logits))
            log1p = jnp.log(1.0 + small)
            part = jnp.exp(jnp.minimum(logits, 0.0) - log1p) * weight
            if tc == 0:
                part = jnp.where(positive, -part, part)
            coef[:, tc * TILE : (tc + 1) * TILE] = part.astype(jnp.bfloat16)
            exact = jnp.where(small < 2.0**-9, small * (1.0 - 0.5 * small), log1p)
            terms = jnp.maximum(logits, 0.0) + exact
            loss_acc[...] += jnp.sum(terms.reshape(TILE // 8, 8, TILE), axis=0)
        c = coef[...]
        grad = jnp.dot(c, texts[...], preferred_element_type=jnp.float32)

        @pl.when(ic == 0)
        def _():
            gi_wide[...] = grad[:rows]

        gi_stage[at, :] = encode(grad)
        for tc in range(total // TILE):
            place = slice(tc * TILE, (tc + 1) * TILE)
            text_acc[place, :] += lax.dot_general(
                c[:, place], left, (((0,), (0,)), ((), ())), preferred_element_type=jnp.float32
            )
        return 0

    lax.fori_loop(0, total // TILE, step, 0)
    loss_ref[...] = loss_acc[...]
    copies = [pltpu.make_async_copy(gi_wide, gi_own, out_sems.at[0])]
    for i in range(7):
        copies.append(pltpu.make_async_copy(gi_stage.at[pl.ds((i + 1) * rows, rows), :], gi_codes[i], out_sems.at[1 + i]))
    for i in range(4):
        copies.append(pltpu.make_async_copy(text_acc.at[pl.ds(i * rows, rows), :], gt_wide[i], out_sems.at[8 + i]))
    for i in range(4):
        gt_stage[i * rows : (i + 1) * rows, :] = encode(text_acc[(4 + i) * rows : (5 + i) * rows, :])
        copies.append(pltpu.make_async_copy(gt_stage.at[pl.ds(i * rows, rows), :], gt_codes[i], out_sems.at[12 + i]))
    for copy in copies:
        copy.start()
    for copy in copies:
        copy.wait()


def multiply(scalars, image_shares, text_shares):
    rows, width = image_shares[0].shape
    total = 8 * rows
    any_space = pl.BlockSpec(memory_space=pl.ANY)
    wide = jax.ShapeDtypeStruct((rows, width), jnp.float32)
    code = jax.ShapeDtypeStruct((rows, width), jnp.bfloat16)
    return pl.pallas_call(
        kernel,
        out_shape=[wide] + [code] * 7 + [wide] * 4 + [code] * 4 + [jax.ShapeDtypeStruct((8, TILE), jnp.float32)],
        in_specs=[pl.BlockSpec(memory_space=pltpu.SMEM)] + [any_space] * 16,
        out_specs=[any_space] * 16 + [pl.BlockSpec(memory_space=pltpu.VMEM)],
        scratch_shapes=[
            pltpu.VMEM((total, width), jnp.bfloat16),
            pltpu.VMEM((total, width), jnp.bfloat16),
            pltpu.VMEM((total, width), jnp.float32),
            pltpu.VMEM((TILE, total), jnp.bfloat16),
            pltpu.VMEM((rows, width), jnp.float32),
            pltpu.VMEM((total, width), jnp.bfloat16),
            pltpu.VMEM((4 * rows, width), jnp.bfloat16),
            pltpu.VMEM((8, TILE), jnp.float32),
            pltpu.SemaphoreType.DMA((16,)),
            pltpu.SemaphoreType.DMA((16,)),
        ],
        compiler_params=pltpu.CompilerParams(vmem_limit_bytes=40 * 1024 * 1024),
        cost_estimate=pl.CostEstimate(
            flops=6 * total * total * width, bytes_accessed=16 * total * width, transcendentals=3 * total * total
        ),
        name="pairs",
    )(scalars, *image_shares, *text_shares)


def body(images, texts, logit_scale, logit_bias):
    rows, width = images.shape
    core = lax.axis_index("blk") % 2
    factor = logit_scale[0] / math.sqrt(width)
    weight = factor / math.sqrt(STEPS * 8 * rows)
    scalars = jnp.stack([factor, logit_bias[0], weight])

    across = shift_group(images, 1, 0)
    behind1 = shift_blk(texts, 2, 2)
    behind2 = shift_blk(texts, 4, 4)
    direct = [shift_group(images, 0, d) for d in (1, -1, 2)]
    relayed = [shift_group(across, 0, d) for d in (1, -1, 2)]
    behind3 = shift_blk(behind1, 4, 4)
    extra = shift_blk(jnp.where(core == 0, texts, behind2), 1, 3)
    siblings = [swap_core(b) for b in (behind1, behind2, behind3)]
    image_shares = [images, across] + direct + relayed
    text_shares = [texts, behind1, behind2, behind3, extra] + siblings
    out = multiply(scalars, image_shares, text_shares)
    gi_own, gi_codes = out[0], out[1:8]
    gt_own, gt1, gt2, gt3 = out[8:12]
    gt_extra, gt_sib1, gt_sib2, gt_sib3 = out[12:16]

    loss = jnp.sum(out[16]).reshape(1, 1)

    gt3 = gt3 + decode(swap_core(gt_sib3))
    from3 = shift_blk(encode(gt3), -4, -4)
    from_extra = decode(shift_blk(gt_extra, -3, -1))
    gt1 = gt1 + decode(swap_core(gt_sib1)) + decode(from3)
    gt2 = gt2 + decode(swap_core(gt_sib2)) + jnp.where(core == 1, from_extra, 0.0)
    from1 = shift_blk(encode(gt1), -2, -2)
    from2 = shift_blk(encode(gt2), -4, -4)

    moves = [(1, 0)] + [(0, -d) for d in (1, -1, 2)] + [(1, -d) for d in (1, -1, 2)]
    back = [shift_group(g, y, x) for g, (y, x) in zip(gi_codes, moves)]

    loss = sum_over(loss, "group", 1, 8)
    loss = sum_over(loss, "blk", 4, 8)
    loss = sum_over(loss, "blk", 1, 4)
    pairs = rows * lax.axis_size("group") * lax.axis_size("blk")
    loss = loss.reshape(1) / pairs

    grad_texts = gt_own + jnp.where(core == 0, from_extra, 0.0) + decode(from1) + decode(from2)
    grad_images = gi_own
    for code in back:
        grad_images = grad_images + decode(code)
    return (grad_images, grad_texts, loss)


def solution(mesh):
    return jax.shard_map(
        body,
        mesh=mesh,
        in_specs=(P(("blk", "group"), None), P(("blk", "group"), None), P(), P()),
        out_specs=(P(("blk", "group"), None), P(("blk", "group"), None), P()),
        check_vma=False,
    )
```

```python
import math

import jax
import jax.numpy as jnp
from jax import lax
from jax.experimental import pallas as pl
from jax.experimental.pallas import tpu as pltpu
from jax.sharding import PartitionSpec as P

STEPS = 8
TILE = 256
VMEM_LIMIT = 60 * 1024 * 1024
CODE_SCALE = 2.0**56
CODE_FLOOR = 2.0**-126
HINT = pl.CostEstimate(flops=1, bytes_accessed=1, transcendentals=0)


def encode(value):
    scaled = value * CODE_SCALE
    return (scaled * jnp.abs(scaled)).astype(jnp.bfloat16)


def decode(code):
    wide = code.astype(jnp.float32)
    return wide * lax.rsqrt(jnp.maximum(jnp.abs(wide), CODE_FLOOR)) * (1.0 / CODE_SCALE)


def shift_blk(value, even, odd, name):
    count = lax.axis_size("blk")
    pairs = [(s, (s + (odd if s % 2 else even)) % count) for s in range(count)]
    with jax.named_scope(name):
        return lax.ppermute(value, "blk", pairs)


def swap_core(value, name):
    return shift_blk(value, 1, -1, name)


def swap_y(value, name):
    with jax.named_scope(name):
        return lax.ppermute(value, "group", [(s, (s + 4) % 8) for s in range(8)])


def ring_x(value, steps, name):
    pairs = []
    for b in range(lax.axis_size("blk")):
        for g in range(8):
            x = g % 4 + (-steps if b % 2 else steps)
            pairs.append((b * 8 + g, b * 8 + g // 4 * 4 + x % 4))
    with jax.named_scope(name):
        return lax.ppermute(value, ("blk", "group"), pairs)


def sum_over(value, axis):
    copies = jnp.broadcast_to(value[None], (lax.axis_size(axis), *value.shape))
    with jax.named_scope(f"loss_{axis}"):
        return jnp.sum(lax.all_to_all(copies, axis, 0, 0), axis=0)


def after(value, *others):
    return lax.optimization_barrier((value, *others))[0]


def any_specs(count):
    return [pl.BlockSpec(memory_space=pl.ANY)] * count


def params():
    return pltpu.CompilerParams(vmem_limit_bytes=VMEM_LIMIT)


def fetch_all(pairs, sems):
    copies = [pltpu.make_async_copy(source, target, sems.at[i]) for i, (source, target) in enumerate(pairs)]
    for c in copies:
        c.start()
    return copies


def share_slots(refs, place):
    rows = refs[0].shape[0]
    return [(r, place.at[pl.ds(i * rows, rows), :]) for i, r in enumerate(refs)]


def pairs_kernel(scale, bias_ref, *refs):
    image_refs, text_refs = refs[:8], refs[8:16]
    coef_ref, loss_ref, outs = refs[16], refs[17], refs[18:23]
    images, texts, coef, acc, stage, loss_acc, in_sems, out_sems = refs[23:]
    rows, width = image_refs[0].shape
    total = 8 * rows
    factor = scale[0] * (1.0 / math.sqrt(width))
    weight = factor * (1.0 / math.sqrt(STEPS * total))
    bias = bias_ref[0]
    slots = share_slots(text_refs, texts) + share_slots(image_refs, images)
    copies = [pltpu.make_async_copy(source, target, in_sems.at[i]) for i, (source, target) in enumerate(slots)]
    for i in (0, 1, 10, 11, 2, 3, 4, 5, 6, 7, 12, 13, 14, 15, 8, 9):
        copies[i].start()
    waited = set()
    sends = []
    loss_acc[...] = jnp.zeros_like(loss_acc)
    for it in (1, 2, 3, 0):
        place = pl.ds(it * TILE, TILE)
        for jt in range(total // TILE):
            for i in (8 + 2 * it, 9 + 2 * it, 2 * jt, 2 * jt + 1):
                if i not in waited:
                    copies[i].wait()
                    waited.add(i)
            left = images[place, :]
            right = texts[jt * TILE : (jt + 1) * TILE, :]
            logits = lax.dot_general(left, right, (((1,), (1,)), ((), ())), preferred_element_type=jnp.float32)
            logits = logits * factor + bias
            mixed = it == 0 and jt == 0
            if mixed:
                row = lax.broadcasted_iota(jnp.int32, (TILE, TILE), 0)
                col = lax.broadcasted_iota(jnp.int32, (TILE, TILE), 1)
                positive = jnp.logical_and(row == col, col < rows)
                logits = jnp.where(positive, -logits, logits)
            small = jnp.exp(-jnp.abs(logits))
            log1p = jnp.log(1.0 + small)
            part = jnp.exp(jnp.minimum(logits, 0.0) - log1p) * weight
            if mixed:
                part = jnp.where(positive, -part, part)
            coef[place, jt * TILE : (jt + 1) * TILE] = part.astype(jnp.bfloat16)
            exact = jnp.where(small < 2.0**-9, small * (1.0 - 0.5 * small), log1p)
            terms = jnp.maximum(logits, 0.0) + exact
            loss_acc[...] += jnp.sum(terms.reshape(TILE // 8, 8, TILE), axis=0)
        sends.append(pltpu.make_async_copy(coef.at[place, :], coef_ref.at[place, :], out_sems.at[5 + it]))
        sends[-1].start()
        product = jnp.dot(coef[place, :], texts[...], preferred_element_type=jnp.float32)
        if it == 0:
            acc[...] = product
            for i in range(2):
                sends.append(pltpu.make_async_copy(acc.at[pl.ds(i * rows, rows), :], outs[i], out_sems.at[i]))
                sends[-1].start()
        else:
            stage[place, :] = encode(product)
            sends.append(pltpu.make_async_copy(stage.at[place, :], outs[1 + it], out_sems.at[1 + it]))
            sends[-1].start()
    loss_ref[...] = loss_acc[:, : TILE // 2] + loss_acc[:, TILE // 2 :]
    for s in sends:
        s.wait()


def pairs_part(logit_scale, logit_bias, image_shares, text_shares):
    rows, width = image_shares[0].shape
    total = 8 * rows
    wide = jax.ShapeDtypeStruct((rows, width), jnp.float32)
    return pl.pallas_call(
        pairs_kernel,
        out_shape=[jax.ShapeDtypeStruct((total, total), jnp.bfloat16), jax.ShapeDtypeStruct((8, TILE // 2), jnp.float32)]
        + [wide] * 2
        + [jax.ShapeDtypeStruct((TILE, width), jnp.bfloat16)] * 3,
        in_specs=[pl.BlockSpec(memory_space=pltpu.SMEM)] * 2 + any_specs(16),
        out_specs=any_specs(1) + [pl.BlockSpec(memory_space=pltpu.VMEM)] + any_specs(5),
        scratch_shapes=[
            pltpu.VMEM((total, width), jnp.bfloat16),
            pltpu.VMEM((total, width), jnp.bfloat16),
            pltpu.VMEM((total, total), jnp.bfloat16),
            pltpu.VMEM((TILE, width), jnp.float32),
            pltpu.VMEM((total, width), jnp.bfloat16),
            pltpu.VMEM((8, TILE), jnp.float32),
            pltpu.SemaphoreType.DMA((16,)),
            pltpu.SemaphoreType.DMA((9,)),
        ],
        compiler_params=params(),
        cost_estimate=HINT,
        name="pairs_part",
    )(logit_scale, logit_bias, *image_shares, *text_shares)


def texts_kernel(coef_ref, *refs):
    image_refs, outs = refs[:8], refs[8:16]
    images, coef, acc, stage, in_sems, out_sems = refs[16:]
    rows = image_refs[0].shape[0]
    tiles = 8 * rows // TILE
    order = (2, 3, 1, 0)
    copies = [
        pltpu.make_async_copy(source, target, in_sems.at[i])
        for i, (source, target) in enumerate(
            [(coef_ref.at[:, pl.ds(i * TILE, TILE)], coef.at[:, pl.ds(i * TILE, TILE)]) for i in range(tiles)]
            + share_slots(image_refs, images)
        )
    ]
    for i in (order[0], *range(tiles, tiles + 8), *order[1:]):
        copies[i].start()
    for c in copies[tiles:]:
        c.wait()
    sends = []
    for jt in order:
        copies[jt].wait()
        place = slice(jt * TILE, (jt + 1) * TILE)
        acc[place, :] = lax.dot_general(
            coef[:, place], images[...], (((0,), (0,)), ((), ())), preferred_element_type=jnp.float32
        )
        for i in (2 * jt, 2 * jt + 1):
            part = pl.ds(i * rows, rows)
            if i < 7:
                sends.append(pltpu.make_async_copy(acc.at[part, :], outs[i], out_sems.at[i]))
            else:
                stage[...] = encode(acc[part, :])
                sends.append(pltpu.make_async_copy(stage, outs[i], out_sems.at[i]))
            sends[-1].start()
    for s in sends:
        s.wait()


def texts_part(coef, image_shares):
    rows, width = image_shares[0].shape
    total = 8 * rows
    wide = jax.ShapeDtypeStruct((rows, width), jnp.float32)
    return pl.pallas_call(
        texts_kernel,
        out_shape=[wide] * 7 + [jax.ShapeDtypeStruct((rows, width), jnp.bfloat16)],
        in_specs=any_specs(9),
        out_specs=any_specs(8),
        scratch_shapes=[
            pltpu.VMEM((total, width), jnp.bfloat16),
            pltpu.VMEM((total, total), jnp.bfloat16),
            pltpu.VMEM((total, width), jnp.float32),
            pltpu.VMEM((rows, width), jnp.bfloat16),
            pltpu.SemaphoreType.DMA((12,)),
            pltpu.SemaphoreType.DMA((8,)),
        ],
        compiler_params=params(),
        cost_estimate=HINT,
        name="texts_part",
    )(coef, *image_shares)


def body(images, texts, logit_scale, logit_bias):
    rows, width = images.shape
    core = lax.axis_index("blk") % 2
    across = swap_y(images, "across")
    behind2 = shift_blk(texts, 4, 4, "behind2")
    behind1 = shift_blk(texts, 2, 2, "behind1")
    near = [images]
    far = [across]
    for name, group in (("near", near), ("far", far)):
        first = ring_x(group[0], 1, f"{name}1")
        group += [first, ring_x(first, 1, f"{name}2"), ring_x(group[0], 3, f"{name}3")]
    extra = shift_blk(jnp.where(core == 0, texts, behind2), 1, 3, "extra")
    behind3 = shift_blk(behind2, 2, 2, "behind3")
    sib1, sib2, sib3 = [swap_core(b, "sibling") for b in (behind1, behind2, behind3)]
    image_shares = [s for pair in zip(near, far) for s in pair]
    text_shares = [texts, behind1, behind2, behind3, sib1, sib2, sib3, extra]

    coef, loss, gi_own, gi_across, *gi_codes = pairs_part(logit_scale, logit_bias, image_shares, text_shares)
    back = [ring_x(code, -(i + 1), f"back_x{i + 1}") for i, code in enumerate(gi_codes)]
    gt_own, gt1, gt2, gt3, gt_sib1, gt_sib2, gt_sib3, gt_extra = texts_part(coef, image_shares)

    gt1 = gt1 + swap_core(gt_sib1, "back_sib1")
    gt2 = gt2 + swap_core(gt_sib2, "back_sib2")
    gt3 = gt3 + swap_core(gt_sib3, "back_sib3")
    code13 = jnp.concatenate([encode(gt1), encode(gt3)])
    from_extra = decode(shift_blk(gt_extra, -3, -1, "back_extra"))
    gt2 = gt2 + jnp.where(core == 1, from_extra, 0.0)
    code13, gt2, from_extra = lax.optimization_barrier((code13, gt2, from_extra))
    from13 = shift_blk(code13, -2, -2, "back13")
    code2 = encode(gt2 + decode(from13[rows:]))
    from2 = shift_blk(code2, -4, -4, "back2")

    for code in back:
        gi_own = gi_own + decode(code[:rows])
        gi_across = gi_across + decode(code[rows:])
    code_across = encode(gi_across)
    last = swap_y(code_across, "back_across")
    grad_images = gi_own + decode(last)

    loss = sum_over(after(loss, code13), "blk")
    loss = jnp.sum(sum_over(after(loss, code2, code_across), "group"))
    pairs = rows * lax.axis_size("group") * lax.axis_size("blk")
    loss = loss.reshape(1) / pairs

    grad_texts = gt_own + jnp.where(core == 0, from_extra, 0.0) + decode(from13[:rows]) + decode(from2)
    return (grad_images, grad_texts, loss)


def solution(mesh):
    return jax.shard_map(
        body,
        mesh=mesh,
        in_specs=(P(("blk", "group"), None), P(("blk", "group"), None), P(), P()),
        out_specs=(P(("blk", "group"), None), P(("blk", "group"), None), P()),
        check_vma=False,
    )
```

```python
import math

import jax
import jax.numpy as jnp
from jax import lax
from jax.experimental import pallas as pl
from jax.experimental.pallas import tpu as pltpu
from jax.sharding import PartitionSpec as P

STEPS = 8
TILE = 256
VMEM_LIMIT = 60 * 1024 * 1024
CODE_SCALE = 2.0**56
CODE_FLOOR = 2.0**-126
HINT = pl.CostEstimate(flops=1, bytes_accessed=1, transcendentals=0)


def encode(value):
    scaled = value * CODE_SCALE
    return (scaled * jnp.abs(scaled)).astype(jnp.bfloat16)


def decode(code):
    wide = code.astype(jnp.float32)
    return wide * lax.rsqrt(jnp.maximum(jnp.abs(wide), CODE_FLOOR)) * (1.0 / CODE_SCALE)


def shift_blk(value, even, odd, name):
    count = lax.axis_size("blk")
    pairs = [(s, (s + (odd if s % 2 else even)) % count) for s in range(count)]
    with jax.named_scope(name):
        return lax.ppermute(value, "blk", pairs)


def swap_core(value, name):
    return shift_blk(value, 1, -1, name)


def swap_y(value, name):
    with jax.named_scope(name):
        return lax.ppermute(value, "group", [(s, (s + 4) % 8) for s in range(8)])


def ring_x(value, steps, name):
    pairs = []
    for b in range(lax.axis_size("blk")):
        for g in range(8):
            x = g % 4 + (-steps if b % 2 else steps)
            pairs.append((b * 8 + g, b * 8 + g // 4 * 4 + x % 4))
    with jax.named_scope(name):
        return lax.ppermute(value, ("blk", "group"), pairs)


def sum_over(value, axis):
    with jax.named_scope(f"loss_{axis}"):
        return jnp.sum(lax.all_to_all(value, axis, 0, 0), axis=0)


def after(value, *others):
    return lax.optimization_barrier((value, *others))[0]


def any_specs(count):
    return [pl.BlockSpec(memory_space=pl.ANY)] * count


def params():
    return pltpu.CompilerParams(vmem_limit_bytes=VMEM_LIMIT)


def fetch_all(pairs, sems):
    copies = [pltpu.make_async_copy(source, target, sems.at[i]) for i, (source, target) in enumerate(pairs)]
    for c in copies:
        c.start()
    return copies


def share_slots(refs, place):
    rows = refs[0].shape[0]
    return [(r, place.at[pl.ds(i * rows, rows), :]) for i, r in enumerate(refs)]


def pairs_kernel(scale, bias_ref, *refs):
    image_refs, text_refs = refs[:8], refs[8:16]
    loss_ref, wide_refs, code_refs = refs[16], refs[17:19], refs[19:22]
    text_own_ref, text_mid_ref, text_sib_ref, text_extra_ref = refs[22:26]
    images, texts, coef, acc, stage, text_acc, text_stage, loss_acc, in_sems, out_sems = refs[26:]
    rows, width = image_refs[0].shape
    total = 8 * rows
    factor = scale[0] * (1.0 / math.sqrt(width))
    weight = factor * (1.0 / math.sqrt(STEPS * total))
    bias = bias_ref[0]
    slots = share_slots(text_refs, texts) + share_slots(image_refs, images)
    copies = [pltpu.make_async_copy(source, target, in_sems.at[i]) for i, (source, target) in enumerate(slots)]
    for i in (0, 1, 8, 9, 2, 3, 4, 5, 6, 7, 10, 11, 12, 13, 14, 15):
        copies[i].start()
    waited = set()
    sends = []

    def send(source, target):
        sends.append(pltpu.make_async_copy(source, target, out_sems.at[len(sends)]))
        sends[-1].start()

    loss_acc[...] = jnp.zeros_like(loss_acc)
    for it in range(total // TILE):
        place = pl.ds(it * TILE, TILE)
        for jt in range(total // TILE):
            for i in (8 + 2 * it, 9 + 2 * it, 2 * jt, 2 * jt + 1):
                if i not in waited:
                    copies[i].wait()
                    waited.add(i)
            left = images[place, :]
            right = texts[jt * TILE : (jt + 1) * TILE, :]
            logits = lax.dot_general(left, right, (((1,), (1,)), ((), ())), preferred_element_type=jnp.float32)
            logits = logits * factor + bias
            mixed = it == 0 and jt == 0
            if mixed:
                row = lax.broadcasted_iota(jnp.int32, (TILE, TILE), 0)
                col = lax.broadcasted_iota(jnp.int32, (TILE, TILE), 1)
                positive = jnp.logical_and(row == col, col < rows)
                logits = jnp.where(positive, -logits, logits)
            small = jnp.exp(-jnp.abs(logits))
            log1p = jnp.log(1.0 + small)
            part = jnp.exp(jnp.minimum(logits, 0.0) - log1p) * weight
            if mixed:
                part = jnp.where(positive, -part, part)
            coef[place, jt * TILE : (jt + 1) * TILE] = part.astype(jnp.bfloat16)
            exact = jnp.where(small < 2.0**-9, small * (1.0 - 0.5 * small), log1p)
            terms = jnp.maximum(logits, 0.0) + exact
            loss_acc[...] += jnp.sum(terms.reshape(TILE // 8, 8, TILE), axis=0)
        product = jnp.dot(coef[place, :], texts[...], preferred_element_type=jnp.float32)
        parts = [pl.ds(it * TILE + i * rows, rows) for i in range(2)]
        if it == 0:
            acc[...] = product
            for i in range(2):
                send(acc.at[parts[i], :], wide_refs[i])
        else:
            stage[place, :] = encode(product)
            send(stage.at[place, :], code_refs[it - 1])
    loss = loss_acc[:, : TILE // 2] + loss_acc[:, TILE // 2 :]
    loss_ref[...] = jnp.broadcast_to(loss[None], loss_ref.shape)
    for jt in (2, 3, 1, 0):
        place = pl.ds(jt * TILE, TILE)
        text_acc[place, :] = lax.dot_general(
            coef[:, jt * TILE : (jt + 1) * TILE], images[...], (((0,), (0,)), ((), ())), preferred_element_type=jnp.float32
        )
        for i in (2 * jt, 2 * jt + 1):
            part = text_acc.at[pl.ds(i * rows, rows), :]
            if i == 0:
                send(part, text_own_ref)
            elif i < 4:
                send(part, text_mid_ref.at[pl.ds((i - 1) * rows, rows), :])
            elif i < 7:
                send(part, text_sib_ref.at[pl.ds((i - 4) * rows, rows), :])
            else:
                text_stage[...] = encode(part[...])
                send(text_stage, text_extra_ref)
    for s in sends:
        s.wait()


def pairs_part(logit_scale, logit_bias, image_shares, text_shares):
    rows, width = image_shares[0].shape
    total = 8 * rows

    def wide(count):
        return jax.ShapeDtypeStruct((count, width), jnp.float32)

    def code(count):
        return jax.ShapeDtypeStruct((count, width), jnp.bfloat16)

    return pl.pallas_call(
        pairs_kernel,
        out_shape=[
            jax.ShapeDtypeStruct((lax.axis_size("blk"), 8, TILE // 2), jnp.float32),
            wide(rows),
            wide(rows),
            *[code(TILE)] * 3,
            wide(rows),
            wide(3 * rows),
            wide(3 * rows),
            code(rows),
        ],
        in_specs=[pl.BlockSpec(memory_space=pltpu.SMEM)] * 2 + any_specs(16),
        out_specs=[pl.BlockSpec(memory_space=pltpu.VMEM)] + any_specs(9),
        scratch_shapes=[
            pltpu.VMEM((total, width), jnp.bfloat16),
            pltpu.VMEM((total, width), jnp.bfloat16),
            pltpu.VMEM((total, total), jnp.bfloat16),
            pltpu.VMEM((TILE, width), jnp.float32),
            pltpu.VMEM((total, width), jnp.bfloat16),
            pltpu.VMEM((total, width), jnp.float32),
            pltpu.VMEM((rows, width), jnp.bfloat16),
            pltpu.VMEM((8, TILE), jnp.float32),
            pltpu.SemaphoreType.DMA((16,)),
            pltpu.SemaphoreType.DMA((20,)),
        ],
        compiler_params=params(),
        cost_estimate=HINT,
        name="pairs_part",
    )(logit_scale, logit_bias, *image_shares, *text_shares)


def body(images, texts, logit_scale, logit_bias):
    rows, width = images.shape
    core = lax.axis_index("blk") % 2
    across = swap_y(images, "across")
    behind2 = shift_blk(texts, 4, 4, "behind2")
    behind1 = shift_blk(texts, 2, 2, "behind1")
    near = [images]
    far = [across]
    for name, group in (("near", near), ("far", far)):
        one = ring_x(group[0], 1, f"{name}1")
        group += [one, ring_x(one, 1, f"{name}2"), ring_x(group[0], 3, f"{name}3")]
    extra = shift_blk(jnp.where(core == 0, texts, behind2), 1, 3, "extra")
    behind3 = shift_blk(behind2, 2, 2, "behind3")
    sib2 = swap_core(behind2, "sibling2")
    sib1 = swap_core(after(behind1, far[1], near[2]), "sibling1")
    sib3 = swap_core(after(behind3, far[1], near[2]), "sibling3")
    image_shares = [s for pair in zip(near, far) for s in pair]
    text_shares = [texts, behind1, behind3, behind2, sib1, sib3, sib2, extra]

    loss, own, other, *codes, gt_own, gt_mid, gt_sib, gt_extra = pairs_part(
        logit_scale, logit_bias, image_shares, text_shares
    )

    sibling = swap_core(gt_sib, "back_sib")
    back = [ring_x(c, -(i + 1), f"back_x{i + 1}") for i, c in enumerate(codes)]
    code13 = encode(gt_mid[: 2 * rows] + sibling[: 2 * rows])
    from13 = shift_blk(code13, -2, -2, "back13")
    extra_code = shift_blk(after(gt_extra, code13), -3, -1, "back_extra")
    loss = sum_over(after(loss, extra_code), "blk")
    from_extra = decode(extra_code)
    code2 = encode(
        gt_mid[2 * rows :] + sibling[2 * rows :] + jnp.where(core == 1, from_extra, 0.0) + decode(from13[rows:])
    )
    from2 = shift_blk(code2, -4, -4, "back2")
    for code in back:
        other = other + decode(code[rows:])
    other = encode(other)
    last = swap_y(other, "back_across")
    loss = jnp.broadcast_to(loss[None], (lax.axis_size("group"), *loss.shape))
    loss = jnp.sum(sum_over(after(loss, other, code2), "group"))
    for code in back:
        own = own + decode(code[:rows])
    grad_images = own + decode(last)
    grad_texts = gt_own + jnp.where(core == 0, from_extra, 0.0) + decode(from13[:rows]) + decode(from2)
    pairs = rows * lax.axis_size("group") * lax.axis_size("blk")
    loss = loss.reshape(1) / pairs
    return (grad_images, grad_texts, loss)


def solution(mesh):
    return jax.shard_map(
        body,
        mesh=mesh,
        in_specs=(P(("blk", "group"), None), P(("blk", "group"), None), P(), P()),
        out_specs=(P(("blk", "group"), None), P(("blk", "group"), None), P()),
        check_vma=False,
    )
```

```python
import math

import jax
import jax.numpy as jnp
from jax import lax
from jax.experimental import pallas as pl
from jax.experimental.pallas import tpu as pltpu
from jax.sharding import PartitionSpec as P

STEPS = 8
TILE = 256
VMEM_LIMIT = 60 * 1024 * 1024
CODE_SCALE = 2.0**56
CODE_FLOOR = 2.0**-126
HINT = pl.CostEstimate(flops=1, bytes_accessed=1, transcendentals=0)


def encode(value):
    scaled = value * CODE_SCALE
    return (scaled * jnp.abs(scaled)).astype(jnp.bfloat16)


def decode(code):
    wide = code.astype(jnp.float32)
    return wide * lax.rsqrt(jnp.maximum(jnp.abs(wide), CODE_FLOOR)) * (1.0 / CODE_SCALE)


def shift_blk(value, even, odd, name):
    count = lax.axis_size("blk")
    pairs = [(s, (s + (odd if s % 2 else even)) % count) for s in range(count)]
    with jax.named_scope(name):
        return lax.ppermute(value, "blk", pairs)


def swap_core(value, name):
    return shift_blk(value, 1, -1, name)


def flip_y(value, name):
    with jax.named_scope(name):
        return lax.ppermute(value, "blk", [(s, s ^ 2) for s in range(lax.axis_size("blk"))])


def swap_y(value, name):
    with jax.named_scope(name):
        return lax.ppermute(value, "group", [(s, (s + 4) % 8) for s in range(8)])


def ring_x(value, steps, name):
    pairs = []
    for b in range(lax.axis_size("blk")):
        for g in range(8):
            x = g % 4 + (-steps if b % 2 else steps)
            pairs.append((b * 8 + g, b * 8 + g // 4 * 4 + x % 4))
    with jax.named_scope(name):
        return lax.ppermute(value, ("blk", "group"), pairs)


def sum_over(value, axis):
    with jax.named_scope(f"loss_{axis}"):
        return jnp.sum(lax.all_to_all(value, axis, 0, 0), axis=0)


def after(value, *others):
    return lax.optimization_barrier((value, *others))[0]


def any_specs(count):
    return [pl.BlockSpec(memory_space=pl.ANY)] * count


def params():
    return pltpu.CompilerParams(vmem_limit_bytes=VMEM_LIMIT)


def fetch_all(pairs, sems):
    copies = [pltpu.make_async_copy(source, target, sems.at[i]) for i, (source, target) in enumerate(pairs)]
    for c in copies:
        c.start()
    return copies


def share_slots(refs, place):
    rows = refs[0].shape[0]
    return [(r, place.at[pl.ds(i * rows, rows), :]) for i, r in enumerate(refs)]


def pairs_kernel(scale, bias_ref, *refs):
    image_refs, text_refs = refs[:8], refs[8:16]
    loss_ref, wide_refs, code_refs = refs[16], refs[17:19], refs[19:22]
    text_own_ref, text_mid_ref, text_sib_ref, text_extra_ref = refs[22:26]
    images, texts, coef, acc, stage, text_acc, text_stage, loss_acc, in_sems, out_sems = refs[26:]
    rows, width = image_refs[0].shape
    total = 8 * rows
    factor = scale[0] * (1.0 / math.sqrt(width))
    weight = factor * (1.0 / math.sqrt(STEPS * total))
    bias = bias_ref[0]
    slots = share_slots(text_refs, texts) + share_slots(image_refs, images)
    copies = [pltpu.make_async_copy(source, target, in_sems.at[i]) for i, (source, target) in enumerate(slots)]
    for i in (0, 1, 8, 9, 2, 3, 4, 5, 6, 7, 10, 11, 12, 13, 14, 15):
        copies[i].start()
    waited = set()
    sends = []

    def send(source, target):
        sends.append(pltpu.make_async_copy(source, target, out_sems.at[len(sends)]))
        sends[-1].start()

    loss_acc[...] = jnp.zeros_like(loss_acc)
    for it in range(total // TILE):
        place = pl.ds(it * TILE, TILE)
        for jt in range(total // TILE):
            for i in (8 + 2 * it, 9 + 2 * it, 2 * jt, 2 * jt + 1):
                if i not in waited:
                    copies[i].wait()
                    waited.add(i)
            left = images[place, :]
            right = texts[jt * TILE : (jt + 1) * TILE, :]
            logits = lax.dot_general(left, right, (((1,), (1,)), ((), ())), preferred_element_type=jnp.float32)
            logits = logits * factor + bias
            mixed = it == 0 and jt == 0
            if mixed:
                row = lax.broadcasted_iota(jnp.int32, (TILE, TILE), 0)
                col = lax.broadcasted_iota(jnp.int32, (TILE, TILE), 1)
                positive = jnp.logical_and(row == col, col < rows)
                logits = jnp.where(positive, -logits, logits)
            small = jnp.exp(-jnp.abs(logits))
            log1p = jnp.log(1.0 + small)
            part = jnp.exp(jnp.minimum(logits, 0.0) - log1p) * weight
            if mixed:
                part = jnp.where(positive, -part, part)
            coef[place, jt * TILE : (jt + 1) * TILE] = part.astype(jnp.bfloat16)
            exact = jnp.where(small < 2.0**-9, small * (1.0 - 0.5 * small), log1p)
            terms = jnp.maximum(logits, 0.0) + exact
            loss_acc[...] += jnp.sum(terms.reshape(TILE // 8, 8, TILE), axis=0)
        product = jnp.dot(coef[place, :], texts[...], preferred_element_type=jnp.float32)
        parts = [pl.ds(it * TILE + i * rows, rows) for i in range(2)]
        if it == 0:
            acc[...] = product
            for i in range(2):
                send(acc.at[parts[i], :], wide_refs[i])
        else:
            stage[place, :] = encode(product)
            send(stage.at[place, :], code_refs[it - 1])
    loss = loss_acc[:, : TILE // 2] + loss_acc[:, TILE // 2 :]
    loss_ref[...] = jnp.broadcast_to(loss[None], loss_ref.shape)
    for jt in (2, 3, 1, 0):
        place = pl.ds(jt * TILE, TILE)
        text_acc[place, :] = lax.dot_general(
            coef[:, jt * TILE : (jt + 1) * TILE], images[...], (((0,), (0,)), ((), ())), preferred_element_type=jnp.float32
        )
        for i in (2 * jt, 2 * jt + 1):
            part = text_acc.at[pl.ds(i * rows, rows), :]
            if i == 0:
                send(part, text_own_ref)
            elif i < 4:
                send(part, text_mid_ref.at[pl.ds((i - 1) * rows, rows), :])
            elif i < 7:
                send(part, text_sib_ref.at[pl.ds((i - 4) * rows, rows), :])
            else:
                text_stage[...] = encode(part[...])
                send(text_stage, text_extra_ref)
    for s in sends:
        s.wait()


def pairs_part(logit_scale, logit_bias, image_shares, text_shares):
    rows, width = image_shares[0].shape
    total = 8 * rows

    def wide(count):
        return jax.ShapeDtypeStruct((count, width), jnp.float32)

    def code(count):
        return jax.ShapeDtypeStruct((count, width), jnp.bfloat16)

    return pl.pallas_call(
        pairs_kernel,
        out_shape=[
            jax.ShapeDtypeStruct((lax.axis_size("blk"), 8, TILE // 2), jnp.float32),
            wide(rows),
            wide(rows),
            *[code(TILE)] * 3,
            wide(rows),
            wide(3 * rows),
            wide(3 * rows),
            code(rows),
        ],
        in_specs=[pl.BlockSpec(memory_space=pltpu.SMEM)] * 2 + any_specs(16),
        out_specs=[pl.BlockSpec(memory_space=pltpu.VMEM)] + any_specs(9),
        scratch_shapes=[
            pltpu.VMEM((total, width), jnp.bfloat16),
            pltpu.VMEM((total, width), jnp.bfloat16),
            pltpu.VMEM((total, total), jnp.bfloat16),
            pltpu.VMEM((TILE, width), jnp.float32),
            pltpu.VMEM((total, width), jnp.bfloat16),
            pltpu.VMEM((total, width), jnp.float32),
            pltpu.VMEM((rows, width), jnp.bfloat16),
            pltpu.VMEM((8, TILE), jnp.float32),
            pltpu.SemaphoreType.DMA((16,)),
            pltpu.SemaphoreType.DMA((20,)),
        ],
        compiler_params=params(),
        cost_estimate=HINT,
        name="pairs_part",
    )(logit_scale, logit_bias, *image_shares, *text_shares)


def body(images, texts, logit_scale, logit_bias):
    rows, width = images.shape
    core = lax.axis_index("blk") % 2
    half = lax.axis_index("blk") // 2 % 2
    across = swap_y(images, "across")
    behind2 = shift_blk(texts, 4, 4, "behind2")
    behind1 = flip_y(jnp.where(half == 0, texts, behind2), "behind1")
    near = [images]
    far = [across]
    for name, group in (("near", near), ("far", far)):
        one = ring_x(group[0], 1, f"{name}1")
        three = ring_x(group[0], 3, f"{name}3")
        two = ring_x(one if name == "near" else after(one, near[3]), 1, f"{name}2")
        group += [one, two, three]
    extra = shift_blk(jnp.where(core == 0, texts, behind2), 1, 3, "extra")
    behind3 = shift_blk(behind1, 4, 4, "behind3")
    sib2 = swap_core(behind2, "sibling2")
    sib1 = swap_core(behind1, "sibling1")
    sib3 = swap_core(behind3, "sibling3")
    image_shares = [s for pair in zip(near, far) for s in pair]
    text_shares = [texts, behind1, behind3, behind2, sib1, sib3, sib2, extra]

    loss, own, other, *codes, gt_own, gt_mid, gt_sib, gt_extra = pairs_part(
        logit_scale, logit_bias, image_shares, text_shares
    )

    sibling = swap_core(gt_sib, "back_sib")
    back = [ring_x(c, -(i + 1), f"back_x{i + 1}") for i, c in enumerate(codes)]
    code13 = encode(gt_mid[: 2 * rows] + sibling[: 2 * rows])
    from13 = shift_blk(code13, -2, -2, "back13")
    extra_code = shift_blk(after(gt_extra, code13), -3, -1, "back_extra")
    loss = sum_over(after(loss, code13), "blk")
    from_extra = decode(extra_code)
    code2 = encode(
        gt_mid[2 * rows :] + sibling[2 * rows :] + jnp.where(core == 1, from_extra, 0.0) + decode(from13[rows:])
    )
    from2 = shift_blk(code2, -4, -4, "back2")
    for code in back:
        other = other + decode(code[rows:])
    other = encode(other)
    last = swap_y(other, "back_across")
    loss = jnp.broadcast_to(loss[None], (lax.axis_size("group"), *loss.shape))
    loss = jnp.sum(sum_over(after(loss, other, code2), "group"))
    for code in back:
        own = own + decode(code[:rows])
    grad_images = own + decode(last)
    grad_texts = gt_own + jnp.where(core == 0, from_extra, 0.0) + decode(from13[:rows]) + decode(from2)
    pairs = rows * lax.axis_size("group") * lax.axis_size("blk")
    loss = loss.reshape(1) / pairs
    return (grad_images, grad_texts, loss)


def solution(mesh):
    return jax.shard_map(
        body,
        mesh=mesh,
        in_specs=(P(("blk", "group"), None), P(("blk", "group"), None), P(), P()),
        out_specs=(P(("blk", "group"), None), P(("blk", "group"), None), P()),
        check_vma=False,
    )
```

```python
import math

import jax
import jax.numpy as jnp
from jax import lax
from jax.experimental import pallas as pl
from jax.experimental.pallas import tpu as pltpu
from jax.sharding import PartitionSpec as P

STEPS = 8
TILE = 256
VMEM_LIMIT = 60 * 1024 * 1024
CODE_SCALE = 2.0**56
CODE_FLOOR = 2.0**-126
HINT = pl.CostEstimate(flops=1, bytes_accessed=1, transcendentals=0)


def encode(value):
    scaled = value * CODE_SCALE
    return (scaled * jnp.abs(scaled)).astype(jnp.bfloat16)


def decode(code):
    wide = code.astype(jnp.float32)
    return wide * lax.rsqrt(jnp.maximum(jnp.abs(wide), CODE_FLOOR)) * (1.0 / CODE_SCALE)


def shift_blk(value, even, odd, name):
    count = lax.axis_size("blk")
    pairs = [(s, (s + (odd if s % 2 else even)) % count) for s in range(count)]
    with jax.named_scope(name):
        return lax.ppermute(value, "blk", pairs)


def swap_core(value, name):
    return shift_blk(value, 1, -1, name)


def flip_y(value, name):
    with jax.named_scope(name):
        return lax.ppermute(value, "blk", [(s, s ^ 2) for s in range(lax.axis_size("blk"))])


def swap_y(value, name):
    with jax.named_scope(name):
        return lax.ppermute(value, "group", [(s, (s + 4) % 8) for s in range(8)])


def ring_x(value, steps, name):
    pairs = []
    for b in range(lax.axis_size("blk")):
        for g in range(8):
            x = g % 4 + (-steps if b % 2 else steps)
            pairs.append((b * 8 + g, b * 8 + g // 4 * 4 + x % 4))
    with jax.named_scope(name):
        return lax.ppermute(value, ("blk", "group"), pairs)


def sum_over(value, axis):
    with jax.named_scope(f"loss_{axis}"):
        return jnp.sum(lax.all_to_all(value, axis, 0, 0), axis=0)


def after(value, *others):
    return lax.optimization_barrier((value, *others))[0]


def any_specs(count):
    return [pl.BlockSpec(memory_space=pl.ANY)] * count


def params():
    return pltpu.CompilerParams(vmem_limit_bytes=VMEM_LIMIT)


def fetch_all(pairs, sems):
    copies = [pltpu.make_async_copy(source, target, sems.at[i]) for i, (source, target) in enumerate(pairs)]
    for c in copies:
        c.start()
    return copies


def share_slots(refs, place):
    rows = refs[0].shape[0]
    return [(r, place.at[pl.ds(i * rows, rows), :]) for i, r in enumerate(refs)]


def pairs_kernel(scale, bias_ref, *refs):
    image_refs, text_refs = refs[:8], refs[8:16]
    loss_ref, wide_refs, code_refs = refs[16], refs[17:19], refs[19:22]
    text_own_ref, text_mid_ref, text_sib_ref, text_extra_ref = refs[22:26]
    images, texts, coef, acc, stage, text_acc, text_stage, loss_acc, in_sems, out_sems = refs[26:]
    rows, width = image_refs[0].shape
    total = 8 * rows
    factor = scale[0] * (1.0 / math.sqrt(width))
    weight = factor * (1.0 / math.sqrt(STEPS * total))
    bias = bias_ref[0]
    slots = share_slots(text_refs, texts) + share_slots(image_refs, images)
    copies = [pltpu.make_async_copy(source, target, in_sems.at[i]) for i, (source, target) in enumerate(slots)]
    for i in (0, 1, 8, 9, 2, 3, 4, 5, 6, 7, 10, 11, 12, 13, 14, 15):
        copies[i].start()
    waited = set()
    sends = []

    def send(source, target):
        sends.append(pltpu.make_async_copy(source, target, out_sems.at[len(sends)]))
        sends[-1].start()

    loss_acc[...] = jnp.zeros_like(loss_acc)
    for it in range(total // TILE):
        place = pl.ds(it * TILE, TILE)
        for jt in range(total // TILE):
            for i in (8 + 2 * it, 9 + 2 * it, 2 * jt, 2 * jt + 1):
                if i not in waited:
                    copies[i].wait()
                    waited.add(i)
            left = images[place, :]
            right = texts[jt * TILE : (jt + 1) * TILE, :]
            logits = lax.dot_general(left, right, (((1,), (1,)), ((), ())), preferred_element_type=jnp.float32)
            logits = logits * factor + bias
            mixed = it == 0 and jt == 0
            if mixed:
                row = lax.broadcasted_iota(jnp.int32, (TILE, TILE), 0)
                col = lax.broadcasted_iota(jnp.int32, (TILE, TILE), 1)
                positive = jnp.logical_and(row == col, col < rows)
                logits = jnp.where(positive, -logits, logits)
            small = jnp.exp(-jnp.abs(logits))
            log1p = jnp.log(1.0 + small)
            exact = jnp.where(small < 2.0**-9, small * (1.0 - 0.5 * small), log1p)
            terms = jnp.maximum(logits, 0.0) + exact
            part = jnp.exp(logits - terms) * weight
            if mixed:
                part = jnp.where(positive, -part, part)
            coef[place, jt * TILE : (jt + 1) * TILE] = part.astype(jnp.bfloat16)
            loss_acc[...] += jnp.sum(terms.reshape(TILE // 8, 8, TILE), axis=0)
        product = jnp.dot(coef[place, :], texts[...], preferred_element_type=jnp.float32)
        parts = [pl.ds(it * TILE + i * rows, rows) for i in range(2)]
        if it == 0:
            acc[...] = product
            for i in range(2):
                send(acc.at[parts[i], :], wide_refs[i])
        else:
            stage[place, :] = encode(product)
            send(stage.at[place, :], code_refs[it - 1])
    loss = loss_acc[:, : TILE // 2] + loss_acc[:, TILE // 2 :]
    loss_ref[...] = jnp.broadcast_to(loss[None], loss_ref.shape)
    for jt in (2, 3, 1, 0):
        place = pl.ds(jt * TILE, TILE)
        text_acc[place, :] = lax.dot_general(
            coef[:, jt * TILE : (jt + 1) * TILE], images[...], (((0,), (0,)), ((), ())), preferred_element_type=jnp.float32
        )
        for i in (2 * jt, 2 * jt + 1):
            part = text_acc.at[pl.ds(i * rows, rows), :]
            if i == 0:
                send(part, text_own_ref)
            elif i < 4:
                send(part, text_mid_ref.at[pl.ds((i - 1) * rows, rows), :])
            elif i < 7:
                send(part, text_sib_ref.at[pl.ds((i - 4) * rows, rows), :])
            else:
                text_stage[...] = encode(part[...])
                send(text_stage, text_extra_ref)
    for s in sends:
        s.wait()


def pairs_part(logit_scale, logit_bias, image_shares, text_shares):
    rows, width = image_shares[0].shape
    total = 8 * rows

    def wide(count):
        return jax.ShapeDtypeStruct((count, width), jnp.float32)

    def code(count):
        return jax.ShapeDtypeStruct((count, width), jnp.bfloat16)

    return pl.pallas_call(
        pairs_kernel,
        out_shape=[
            jax.ShapeDtypeStruct((lax.axis_size("blk"), 8, TILE // 2), jnp.float32),
            wide(rows),
            wide(rows),
            *[code(TILE)] * 3,
            wide(rows),
            wide(3 * rows),
            wide(3 * rows),
            code(rows),
        ],
        in_specs=[pl.BlockSpec(memory_space=pltpu.SMEM)] * 2 + any_specs(16),
        out_specs=[pl.BlockSpec(memory_space=pltpu.VMEM)] + any_specs(9),
        scratch_shapes=[
            pltpu.VMEM((total, width), jnp.bfloat16),
            pltpu.VMEM((total, width), jnp.bfloat16),
            pltpu.VMEM((total, total), jnp.bfloat16),
            pltpu.VMEM((TILE, width), jnp.float32),
            pltpu.VMEM((total, width), jnp.bfloat16),
            pltpu.VMEM((total, width), jnp.float32),
            pltpu.VMEM((rows, width), jnp.bfloat16),
            pltpu.VMEM((8, TILE), jnp.float32),
            pltpu.SemaphoreType.DMA((16,)),
            pltpu.SemaphoreType.DMA((20,)),
        ],
        compiler_params=params(),
        cost_estimate=HINT,
        name="pairs_part",
    )(logit_scale, logit_bias, *image_shares, *text_shares)


def body(images, texts, logit_scale, logit_bias):
    rows, width = images.shape
    core = lax.axis_index("blk") % 2
    half = lax.axis_index("blk") // 2 % 2
    across = swap_y(images, "across")
    behind2 = shift_blk(texts, 4, 4, "behind2")
    behind1 = flip_y(jnp.where(half == 0, texts, behind2), "behind1")
    near = [images]
    far = [across]
    for name, group in (("near", near), ("far", far)):
        start = group[0] if name == "near" else after(group[0], near[1], near[3])
        one = ring_x(start, 1, f"{name}1")
        three = ring_x(start, 3, f"{name}3")
        two = ring_x(after(one, three if name == "near" else near[3]), 1, f"{name}2")
        group += [one, two, three]
    extra = shift_blk(jnp.where(core == 0, texts, behind2), 1, 3, "extra")
    behind3 = shift_blk(behind1, 4, 4, "behind3")
    sib2 = swap_core(behind2, "sibling2")
    sib1 = swap_core(behind1, "sibling1")
    sib3 = swap_core(behind3, "sibling3")
    image_shares = [s for pair in zip(near, far) for s in pair]
    text_shares = [texts, behind1, behind3, behind2, sib1, sib3, sib2, extra]

    loss, own, other, *codes, gt_own, gt_mid, gt_sib, gt_extra = pairs_part(
        logit_scale, logit_bias, image_shares, text_shares
    )

    sibling = swap_core(gt_sib, "back_sib")
    back = [ring_x(c, -(i + 1), f"back_x{i + 1}") for i, c in enumerate(codes)]
    code13 = encode(gt_mid[: 2 * rows] + sibling[: 2 * rows])
    from13 = shift_blk(code13, -2, -2, "back13")
    extra_code = shift_blk(after(gt_extra, code13), -3, -1, "back_extra")
    loss = sum_over(after(loss, code13), "blk")
    from_extra = decode(extra_code)
    code2 = encode(
        gt_mid[2 * rows :] + sibling[2 * rows :] + jnp.where(core == 1, from_extra, 0.0) + decode(from13[rows:])
    )
    from2 = shift_blk(code2, -4, -4, "back2")
    for code in back:
        other = other + decode(code[rows:])
    other = encode(other)
    last = swap_y(other, "back_across")
    loss = jnp.broadcast_to(loss[None], (lax.axis_size("group"), *loss.shape))
    loss = jnp.sum(sum_over(after(loss, other, code2), "group"))
    for code in back:
        own = own + decode(code[:rows])
    grad_images = own + decode(last)
    grad_texts = gt_own + jnp.where(core == 0, from_extra, 0.0) + decode(from13[:rows]) + decode(from2)
    pairs = rows * lax.axis_size("group") * lax.axis_size("blk")
    loss = loss.reshape(1) / pairs
    return (grad_images, grad_texts, loss)


def solution(mesh):
    return jax.shard_map(
        body,
        mesh=mesh,
        in_specs=(P(("blk", "group"), None), P(("blk", "group"), None), P(), P()),
        out_specs=(P(("blk", "group"), None), P(("blk", "group"), None), P()),
        check_vma=False,
    )
```

```python
import math

import jax
import jax.numpy as jnp
from jax import lax
from jax.experimental import pallas as pl
from jax.experimental.pallas import tpu as pltpu
from jax.sharding import PartitionSpec as P

STEPS = 8
TILE = 256
VMEM_LIMIT = 60 * 1024 * 1024
CODE_SCALE = 2.0**56
CODE_FLOOR = 2.0**-126
HINT = pl.CostEstimate(flops=1, bytes_accessed=1, transcendentals=0)


def encode(value):
    scaled = value * CODE_SCALE
    return (scaled * jnp.abs(scaled)).astype(jnp.bfloat16)


def decode(code):
    wide = code.astype(jnp.float32)
    return wide * lax.rsqrt(jnp.maximum(jnp.abs(wide), CODE_FLOOR)) * (1.0 / CODE_SCALE)


def shift_blk(value, even, odd, name):
    count = lax.axis_size("blk")
    pairs = [(s, (s + (odd if s % 2 else even)) % count) for s in range(count)]
    with jax.named_scope(name):
        return lax.ppermute(value, "blk", pairs)


def swap_core(value, name):
    return shift_blk(value, 1, -1, name)


def flip_y(value, name):
    with jax.named_scope(name):
        return lax.ppermute(value, "blk", [(s, s ^ 2) for s in range(lax.axis_size("blk"))])


def swap_y(value, name):
    with jax.named_scope(name):
        return lax.ppermute(value, "group", [(s, (s + 4) % 8) for s in range(8)])


def ring_x(value, steps, name):
    pairs = []
    for b in range(lax.axis_size("blk")):
        for g in range(8):
            x = g % 4 + (-steps if b % 2 else steps)
            pairs.append((b * 8 + g, b * 8 + g // 4 * 4 + x % 4))
    with jax.named_scope(name):
        return lax.ppermute(value, ("blk", "group"), pairs)


def sum_over(value, axis):
    with jax.named_scope(f"loss_{axis}"):
        return jnp.sum(lax.all_to_all(value, axis, 0, 0), axis=0)


def after(value, *others):
    return lax.optimization_barrier((value, *others))[0]


def any_specs(count):
    return [pl.BlockSpec(memory_space=pl.ANY)] * count


def params():
    return pltpu.CompilerParams(vmem_limit_bytes=VMEM_LIMIT)


def fetch_all(pairs, sems):
    copies = [pltpu.make_async_copy(source, target, sems.at[i]) for i, (source, target) in enumerate(pairs)]
    for c in copies:
        c.start()
    return copies


def share_slots(refs, place):
    rows = refs[0].shape[0]
    return [(r, place.at[pl.ds(i * rows, rows), :]) for i, r in enumerate(refs)]


def pairs_kernel(scale, bias_ref, *refs):
    image_refs, text_refs = refs[:8], refs[8:16]
    loss_ref, wide_refs, code_refs = refs[16], refs[17:19], refs[19:22]
    text_own_ref, text_mid_ref, text_sib_ref, text_extra_ref = refs[22:26]
    images, texts, coef, acc, stage, text_acc, text_stage, loss_acc, in_sems, out_sems = refs[26:]
    rows, width = image_refs[0].shape
    total = 8 * rows
    factor = scale[0] * (1.0 / math.sqrt(width))
    weight = factor * (1.0 / math.sqrt(STEPS * total))
    bias = bias_ref[0]
    slots = share_slots(text_refs, texts) + share_slots(image_refs, images)
    copies = [pltpu.make_async_copy(source, target, in_sems.at[i]) for i, (source, target) in enumerate(slots)]
    for i in (0, 1, 8, 9, 2, 3, 4, 5, 6, 7, 10, 11, 12, 13, 14, 15):
        copies[i].start()
    waited = set()
    sends = []

    def send(source, target):
        sends.append(pltpu.make_async_copy(source, target, out_sems.at[len(sends)]))
        sends[-1].start()

    loss_acc[...] = jnp.zeros_like(loss_acc)
    for it in range(total // TILE):
        place = pl.ds(it * TILE, TILE)
        for jt in range(total // TILE):
            for i in (8 + 2 * it, 9 + 2 * it, 2 * jt, 2 * jt + 1):
                if i not in waited:
                    copies[i].wait()
                    waited.add(i)
            left = images[place, :]
            right = texts[jt * TILE : (jt + 1) * TILE, :]
            logits = lax.dot_general(left, right, (((1,), (1,)), ((), ())), preferred_element_type=jnp.float32)
            logits = logits * factor + bias
            mixed = it == 0 and jt == 0
            if mixed:
                row = lax.broadcasted_iota(jnp.int32, (TILE, TILE), 0)
                col = lax.broadcasted_iota(jnp.int32, (TILE, TILE), 1)
                positive = jnp.logical_and(row == col, col < rows)
                logits = jnp.where(positive, -logits, logits)
            small = jnp.exp(-jnp.abs(logits))
            log1p = jnp.log(1.0 + small)
            exact = jnp.where(small < 2.0**-9, small * (1.0 - 0.5 * small), log1p)
            terms = jnp.maximum(logits, 0.0) + exact
            part = jnp.exp(logits - terms) * weight
            if mixed:
                part = jnp.where(positive, -part, part)
            coef[place, jt * TILE : (jt + 1) * TILE] = part.astype(jnp.bfloat16)
            loss_acc[...] += jnp.sum(terms.reshape(TILE // 8, 8, TILE), axis=0)
        product = jnp.dot(coef[place, :], texts[...], preferred_element_type=jnp.float32)
        parts = [pl.ds(it * TILE + i * rows, rows) for i in range(2)]
        if it == 0:
            acc[...] = product
            for i in range(2):
                send(acc.at[parts[i], :], wide_refs[i])
        else:
            stage[place, :] = encode(product)
            send(stage.at[place, :], code_refs[it - 1])
    loss = loss_acc[:, : TILE // 2] + loss_acc[:, TILE // 2 :]
    loss_ref[...] = jnp.broadcast_to(loss[None], loss_ref.shape)
    for jt in (2, 3, 1, 0):
        place = pl.ds(jt * TILE, TILE)
        text_acc[place, :] = lax.dot_general(
            coef[:, jt * TILE : (jt + 1) * TILE], images[...], (((0,), (0,)), ((), ())), preferred_element_type=jnp.float32
        )
        for i in (2 * jt, 2 * jt + 1):
            part = text_acc.at[pl.ds(i * rows, rows), :]
            if i == 0:
                send(part, text_own_ref)
            elif i < 4:
                send(part, text_mid_ref.at[pl.ds((i - 1) * rows, rows), :])
            elif i < 7:
                send(part, text_sib_ref.at[pl.ds((i - 4) * rows, rows), :])
            else:
                text_stage[...] = encode(part[...])
                send(text_stage, text_extra_ref)
    for s in sends:
        s.wait()


def pairs_part(logit_scale, logit_bias, image_shares, text_shares):
    rows, width = image_shares[0].shape
    total = 8 * rows

    def wide(count):
        return jax.ShapeDtypeStruct((count, width), jnp.float32)

    def code(count):
        return jax.ShapeDtypeStruct((count, width), jnp.bfloat16)

    return pl.pallas_call(
        pairs_kernel,
        out_shape=[
            jax.ShapeDtypeStruct((lax.axis_size("blk"), 8, TILE // 2), jnp.float32),
            wide(rows),
            wide(rows),
            *[code(TILE)] * 3,
            wide(rows),
            wide(3 * rows),
            wide(3 * rows),
            code(rows),
        ],
        in_specs=[pl.BlockSpec(memory_space=pltpu.SMEM)] * 2 + any_specs(16),
        out_specs=[pl.BlockSpec(memory_space=pltpu.VMEM)] + any_specs(9),
        scratch_shapes=[
            pltpu.VMEM((total, width), jnp.bfloat16),
            pltpu.VMEM((total, width), jnp.bfloat16),
            pltpu.VMEM((total, total), jnp.bfloat16),
            pltpu.VMEM((TILE, width), jnp.float32),
            pltpu.VMEM((total, width), jnp.bfloat16),
            pltpu.VMEM((total, width), jnp.float32),
            pltpu.VMEM((rows, width), jnp.bfloat16),
            pltpu.VMEM((8, TILE), jnp.float32),
            pltpu.SemaphoreType.DMA((16,)),
            pltpu.SemaphoreType.DMA((20,)),
        ],
        compiler_params=params(),
        cost_estimate=HINT,
        name="pairs_part",
    )(logit_scale, logit_bias, *image_shares, *text_shares)


def body(images, texts, logit_scale, logit_bias):
    rows, width = images.shape
    core = lax.axis_index("blk") % 2
    half = lax.axis_index("blk") // 2 % 2
    across = swap_y(images, "across")
    behind2 = shift_blk(texts, 4, 4, "behind2")
    behind1 = flip_y(jnp.where(half == 0, texts, behind2), "behind1")
    near = [images]
    far = [across]
    for name, group in (("near", near), ("far", far)):
        start = group[0] if name == "near" else after(group[0], near[1], near[3])
        one = ring_x(start, 1, f"{name}1")
        three = ring_x(start, 3, f"{name}3")
        two = ring_x(after(one, three if name == "near" else near[3]), 1, f"{name}2")
        group += [one, two, three]
    extra = shift_blk(jnp.where(core == 0, texts, behind2), 1, 3, "extra")
    behind3 = shift_blk(behind1, 4, 4, "behind3")
    sib2 = swap_core(behind2, "sibling2")
    sib1 = swap_core(behind1, "sibling1")
    sib3 = swap_core(behind3, "sibling3")
    image_shares = [s for pair in zip(near, far) for s in pair]
    text_shares = [texts, behind1, behind3, behind2, sib1, sib3, sib2, extra]

    loss, own, other, *codes, gt_own, gt_mid, gt_sib, gt_extra = pairs_part(
        logit_scale, logit_bias, image_shares, text_shares
    )

    sibling = swap_core(gt_sib, "back_sib")
    back = [ring_x(c, -(i + 1), f"back_x{i + 1}") for i, c in enumerate(codes)]
    code13 = encode(gt_mid[: 2 * rows] + sibling[: 2 * rows])
    from13 = shift_blk(code13, -2, -2, "back13")
    extra_code = shift_blk(after(gt_extra, code13), -3, -1, "back_extra")
    loss = sum_over(after(loss, code13), "blk")
    from_extra = decode(extra_code)
    code2 = encode(
        gt_mid[2 * rows :] + sibling[2 * rows :] + jnp.where(core == 1, from_extra, 0.0) + decode(from13[rows:])
    )
    from2 = shift_blk(code2, -4, -4, "back2")
    for code in back:
        other = other + decode(code[rows:])
    other = encode(other)
    last = swap_y(other, "back_across")
    loss = jnp.broadcast_to(loss[None], (lax.axis_size("group"), *loss.shape))
    loss = jnp.sum(sum_over(after(loss, code2), "group"))
    for code in back:
        own = own + decode(code[:rows])
    grad_images = own + decode(last)
    grad_texts = gt_own + jnp.where(core == 0, from_extra, 0.0) + decode(from13[:rows]) + decode(from2)
    pairs = rows * lax.axis_size("group") * lax.axis_size("blk")
    loss = loss.reshape(1) / pairs
    return (grad_images, grad_texts, loss)


def solution(mesh):
    return jax.shard_map(
        body,
        mesh=mesh,
        in_specs=(P(("blk", "group"), None), P(("blk", "group"), None), P(), P()),
        out_specs=(P(("blk", "group"), None), P(("blk", "group"), None), P()),
        check_vma=False,
    )
```
